32 devices in a mesh: parts: 2 (over x), pos: 8 (over z, y), slab: 2 (over core).
Axes of the slice: x: 2, y: 2, z: 4, core: 2. Of those that a mesh axis runs over, the one named last changes fastest.
Arguments:
- obj_real: float32 [8, 2048, 1024], P(('parts', 'slab'), 'pos'), parts along dimension 0, may hold values from 0.5 to 1.5
- obj_imag: float32 [8, 2048, 1024], P(('parts', 'slab'), 'pos'), parts along dimension 0, may hold values from -1.5 to 1.5
- probe: float32 [2, 256, 256], replicated, may hold values from -5 to 5
- taps: float32 [2, 63], replicated, may hold values from -1.3 to 1.3
- intensity: float32 [32, 256, 256], P(('parts', 'pos')), parts along dimension 0, may hold values from 0.25 to 8
- row_off: int32 [32], P(('parts', 'pos')), parts along dimension 0, may hold values from 0 to 255
- col_off: int32 [32], P(('parts', 'pos')), parts along dimension 0, may hold values from 0 to 768
Outputs:
- grad_real: float32 [8, 2048, 1024], P(('parts', 'slab'), 'pos'), parts along dimension 0
- grad_imag: float32 [8, 2048, 1024], P(('parts', 'slab'), 'pos'), parts along dimension 0
The draws below stay inside these ranges and needn't reach their ends.
There are 2 independent parts, one for each index of `parts`. The reference program is written for one: setup_inputs(seed, part) draws one part's arguments, and reference() takes and returns one part's arrays. A program takes and returns all parts, laid end to end along the dimension named above; an argument that names none is the same for every part. Nothing has to cross between parts.
All inputs are finite; a program needn't handle non-finite values.
Results may differ from the reference program's by a relative error of at most 0.0003.
Values sent between devices are 32-bit elements; how exact they have to be, the bound alone decides.
A program may use at most 128 MiB of HBM per device.

```python
import math
import jax
import jax.numpy as jnp
from jax import lax

PROBE = 256
TAPS = 63
POSITIONS_LOCAL = 2
OBJ_COLS = 1024
SLICES = 4
POSITIONS = 16
OBJ_ROWS = 2048
N_POS = 8


def draw_taps(key, part):
    phase_key = jax.random.fold_in(key, 11)
    size_key = jax.random.fold_in(key, 12)
    half = (TAPS - 1) // 2
    offsets = jnp.arange(TAPS, dtype=jnp.float32) - float(half)
    chirp = math.pi / TAPS * offsets * offsets
    jitter = jax.random.uniform(phase_key, (TAPS,), jnp.float32, -0.3, 0.3)
    amplitude = jax.random.uniform(size_key, (TAPS,), jnp.float32, 0.9, 1.1)
    angle = chirp + jitter
    scale = amplitude / math.sqrt(TAPS)
    return jnp.stack([scale * jnp.cos(angle), scale * jnp.sin(angle)], 0).astype(jnp.float32)


def place_ends(entries, key, low, top_value):
    shape = entries.shape
    spot = [jax.random.randint(jax.random.fold_in(key, axis), (), 0, shape[axis]) for axis in range(len(shape))]
    entries = entries.at[tuple(spot)].set(low)
    longest = shape.index(max(shape))
    spot[longest] = (spot[longest] + 1) % shape[longest]
    return entries.at[tuple(spot)].set(top_value)


def steps_of(stream_key, dims, split, low, largest):
    loudness, own = 1.0, jax.random.fold_in(stream_key, 6)
    for axis_at, parts in split:
        heights = jnp.exp(jax.random.uniform(jax.random.fold_in(own, axis_at), (parts,), jnp.float32, low / len(split), largest / len(split)))
        loudness = loudness * jnp.repeat(heights, dims[axis_at] // parts).reshape([-1 if axis == axis_at else 1 for axis in range(len(dims))])
    return loudness


def centred(own_key, dims, deviation, bound, cuts=(), held_as=jnp.bfloat16):
    values = jax.random.normal(own_key, dims, jnp.float32) * deviation
    if len(cuts) > 0:
        values = steps_of(own_key, dims, cuts, -0.22, 0.18) * values
    return jnp.clip(values, min=-bound, max=bound).astype(held_as)


def setup_inputs(seed: int = 0, part: int = 0) -> dict:
    keys = jax.random.split(jax.random.key(seed), 8)
    part_keys = jax.random.split(jax.random.fold_in(keys[7], part), 8)
    return {
        "obj_real": jnp.clip(1.0 + 0.1 * jax.random.normal(part_keys[0], (SLICES, OBJ_ROWS, OBJ_COLS), jnp.float32), 0.5, 1.5),
        "obj_imag": centred(part_keys[1], (SLICES, OBJ_ROWS, OBJ_COLS), 0.3, 1.5, ((0, 2), (1, 8)), jnp.float32),
        "probe": centred(keys[2], (2, PROBE, PROBE), 1.0, 5.0, (), jnp.float32),
        "taps": draw_taps(jax.random.fold_in(keys[7], 71), part),
        "intensity": jnp.clip(jnp.exp(math.log(8.0) - 3.465736 * jax.random.uniform(part_keys[4], (POSITIONS, PROBE, PROBE), jnp.float32) ** steps_of(part_keys[4], (POSITIONS, PROBE, PROBE), ((0, 8),), -0.2, 0.2)), 0.25, 8.0),
        "row_off": place_ends(jax.random.randint(part_keys[5], (POSITIONS,), 0, PROBE), jax.random.fold_in(part_keys[5], 1), 0, PROBE - 1).astype(jnp.int32),
        "col_off": place_ends(jax.random.randint(part_keys[6], (POSITIONS,), 0, OBJ_COLS - PROBE + 1), jax.random.fold_in(part_keys[6], 1), 0, OBJ_COLS - PROBE).astype(jnp.int32),
    }


HIGH = lax.Precision.HIGHEST

def cprod(form, ar, ai, br, bi):

    def mul(left, right):
        return jnp.einsum(form, left, right, precision=HIGH, preferred_element_type=jnp.float32)
    return (mul(ar, br) - mul(ai, bi), mul(ar, bi) + mul(ai, br))

def band(taps, width):
    rows = jnp.arange(width, dtype=jnp.int32)[:, None]
    cols = jnp.arange(width, dtype=jnp.int32)[None, :]
    offset = cols - rows
    half = (taps.shape[1] - 1) // 2
    index = jnp.clip(offset + half, 0, taps.shape[1] - 1)
    inside = jnp.abs(offset) <= half
    return (jnp.where(inside, taps[0][index], 0.0), jnp.where(inside, taps[1][index], 0.0))

def fourier(width):
    steps = jnp.arange(width, dtype=jnp.int32)
    phase = steps[:, None] * steps[None, :] % width
    angle = 2.0 * math.pi / width * phase.astype(jnp.float32)
    norm = 1.0 / math.sqrt(width)
    return (jnp.cos(angle) * norm, -jnp.sin(angle) * norm)

def propagate(kr, ki, xr, xi):
    left = cprod('ij,bjk->bik', kr, ki, xr, xi)
    return cprod('bij,kj->bik', left[0], left[1], kr, ki)

def adjoint_prop(kr, ki, xr, xi):
    left = cprod('ji,bjk->bik', kr, -ki, xr, xi)
    return cprod('bij,jk->bik', left[0], left[1], kr, -ki)

def target_amplitude(exit_wave_real, exit_wave_imaginary, measured_pattern, wave_real, wave_imaginary):
    left = cprod('ij,bjk->bik', wave_real, wave_imaginary, exit_wave_real, exit_wave_imaginary)
    farfield_real, farfield_imaginary = cprod('bij,jk->bik', left[0], left[1], wave_real, wave_imaginary)
    amplitude_residual = farfield_real * farfield_real + farfield_imaginary * farfield_imaginary - measured_pattern
    grad_r = 2.0 * amplitude_residual * farfield_real
    grad_i = 2.0 * amplitude_residual * farfield_imaginary
    back = cprod('ij,bjk->bik', wave_real, -wave_imaginary, grad_r, grad_i)
    return cprod('bij,jk->bik', back[0], back[1], wave_real, -wave_imaginary)

def cut(ext_r, ext_i, rows, cols, width):
    depth = ext_r.shape[0]
    zero = jnp.zeros((), jnp.int32)

    def one(row, col):
        start = (zero, row, col)
        return (lax.dynamic_slice(ext_r, start, (depth, width, width)), lax.dynamic_slice(ext_i, start, (depth, width, width)))
    return jax.vmap(one)(rows, cols)

def forward_pass(src_r, src_i, pat_r, pat_i, kr, ki):
    waves_r, waves_i = ([], [])
    cur_r, cur_i = (src_r, src_i)
    for level in range(pat_r.shape[1]):
        waves_r.append(cur_r)
        waves_i.append(cur_i)
        o_r = pat_r[:, level]
        o_i = pat_i[:, level]
        cur_r, cur_i = propagate(kr, ki, cur_r * o_r - cur_i * o_i, cur_r * o_i + cur_i * o_r)
    return (jnp.stack(waves_r, 1), jnp.stack(waves_i, 1), cur_r, cur_i)

def backward_pass(chirp_real, chirp_imaginary, waves_r, waves_i, pat_r, pat_i, kr, ki):
    depth = pat_r.shape[1]
    terms_r = [None] * depth
    terms_i = [None] * depth
    for level in reversed(range(depth)):
        a_r, a_i = adjoint_prop(kr, ki, chirp_real, chirp_imaginary)
        w_r = waves_r[:, level]
        w_i = waves_i[:, level]
        terms_r[level] = a_r * w_r + a_i * w_i
        terms_i[level] = a_i * w_r - a_r * w_i
        o_r = pat_r[:, level]
        o_i = pat_i[:, level]
        chirp_real, chirp_imaginary = (a_r * o_r + a_i * o_i, a_i * o_r - a_r * o_i)
    return (chirp_real, chirp_imaginary, jnp.stack(terms_r, 1), jnp.stack(terms_i, 1))

def deposit(acc_r, acc_i, term_r, term_i, rows, cols):
    depth, width = (term_r.shape[1], term_r.shape[2])
    zero = jnp.zeros((), jnp.int32)

    def add_one(item, state):
        total_r, total_i = state
        start = (zero, rows[item], cols[item])
        now_r = lax.dynamic_slice(total_r, start, (depth, width, width))
        now_i = lax.dynamic_slice(total_i, start, (depth, width, width))
        total_r = lax.dynamic_update_slice(total_r, now_r + term_r[item], start)
        total_i = lax.dynamic_update_slice(total_i, now_i + term_i[item], start)
        return (total_r, total_i)
    return lax.fori_loop(0, term_r.shape[0], add_one, (acc_r, acc_i))

def reference(obj_real, obj_imag, probe, taps, intensity, row_off, col_off):
    width = PROBE
    kr, ki = band(taps, width)
    wave_real, wave_imaginary = fourier(width)
    ext_r = jnp.concatenate([obj_real, obj_real[:, :width]], axis=1)
    ext_i = jnp.concatenate([obj_imag, obj_imag[:, :width]], axis=1)
    lead_r = jnp.broadcast_to(probe[0], (POSITIONS_LOCAL, width, width))
    lead_i = jnp.broadcast_to(probe[1], (POSITIONS_LOCAL, width, width))

    def group(acc, index):
        first_slice_flag = (index * POSITIONS_LOCAL).astype(jnp.int32)
        rows = index.astype(jnp.int32) * width + lax.dynamic_slice_in_dim(row_off, first_slice_flag, POSITIONS_LOCAL, 0)
        cols = lax.dynamic_slice_in_dim(col_off, first_slice_flag, POSITIONS_LOCAL, 0)
        measured_pattern = lax.dynamic_slice_in_dim(intensity, first_slice_flag, POSITIONS_LOCAL, 0)
        pat_r, pat_i = cut(ext_r, ext_i, rows, cols, width)
        waves_r, waves_i, output_real, output_imaginary = forward_pass(lead_r, lead_i, pat_r, pat_i, kr, ki)
        chirp_real, chirp_imaginary = target_amplitude(output_real, output_imaginary, measured_pattern, wave_real, wave_imaginary)
        chirp_real, chirp_imaginary, term_r, term_i = backward_pass(chirp_real, chirp_imaginary, waves_r, waves_i, pat_r, pat_i, kr, ki)
        return (deposit(acc[0], acc[1], term_r, term_i, rows, cols), None)
    zeros = jnp.zeros((SLICES, OBJ_ROWS + width, OBJ_COLS), jnp.float32)
    (acc_r, acc_i), _ = lax.scan(group, (zeros, zeros), jnp.arange(N_POS, dtype=jnp.int32))
    grad_real = acc_r[:, :OBJ_ROWS].at[:, :width].add(acc_r[:, OBJ_ROWS:])
    grad_imag = acc_i[:, :OBJ_ROWS].at[:, :width].add(acc_i[:, OBJ_ROWS:])
    return (grad_real, grad_imag)
```

```python
import math

import jax
import jax.numpy as jnp
import numpy as np
from jax import lax
from jax.experimental import pallas as pl
from jax.experimental.pallas import tpu as pltpu
from jax.sharding import PartitionSpec as P

F32 = jnp.float32
BF16 = jnp.bfloat16
SMEM = pl.BlockSpec(memory_space=pltpu.SMEM)
VMEM = pl.BlockSpec(memory_space=pltpu.VMEM)


def halves(x):
    high = x.astype(BF16)
    return high, (x - high.astype(F32)).astype(BF16)


def left_mul(high, low, x):
    xh, xl = halves(x)
    left = jnp.concatenate([high, high, low], 1)
    right = jnp.concatenate([xh, xl, xh], 0)
    return jnp.dot(left, right, preferred_element_type=F32)


def right_mul(x, high, low):
    xh, xl = halves(x)
    left = jnp.concatenate([xh, xl, xh], 1)
    right = jnp.concatenate([high, high, low], 0)
    return jnp.dot(left, right, preferred_element_type=F32)


def sandwich(left_h, left_l, xr, xi, right_h, right_l):
    n = xr.shape[0]
    y = left_mul(left_h, left_l, jnp.concatenate([xr, xi], 0))
    z = right_mul(jnp.concatenate([y[:n], y[n:]], 1), right_h, right_l)
    return z[:, :n], z[:, n:]


def fourier_blocks(n):
    steps = np.arange(n)
    angle = 2.0 * math.pi / n * ((steps[:, None] * steps[None, :]) % n)
    norm = 1.0 / math.sqrt(n)
    wr, wi = np.cos(angle) * norm, -np.sin(angle) * norm
    c = np.block([[wr, -wi], [wi, wr]]).astype(np.float32)
    d = np.block([[wr, wi], [-wi, wr]]).astype(np.float32)
    out = []
    for m in (c, d):
        high = m.astype(jnp.bfloat16)
        out += [high, (m - high.astype(np.float32)).astype(jnp.bfloat16)]
    return [jnp.asarray(m) for m in out]


def column_place(col, cols_all, span):
    base = jnp.minimum(col // 128 * 128, cols_all - span)
    return pl.multiple_of(base, 128), col - base


def cut_kernel(cols, obj_r, obj_i, own_s, own_o, halo_s, halo_o):
    n = own_s.shape[-1]
    span = n + 128
    for k, out in enumerate((own_s, own_o, halo_s, halo_o)):
        base, shift = column_place(cols[k], obj_r.shape[-1], span)
        for ri, src in enumerate((obj_r, obj_i)):
            wide = src[0, :, pl.ds(base, span)]
            out[ri, 0] = pltpu.roll(wide, lax.rem(span - shift, span), 1)[:, :n]


def wave_kernel(
    info, own_s, own_o, halo_s, halo_o, probe, ring, intensity, ch, cl, dh, dl,
    term_s, term_o, patch, waves, ah, al, bh, bl,
):
    n = probe.shape[-1]
    depth = own_s.shape[1]
    section, row = info[0], info[1]
    unroll_by = lax.rem(n - row, n)
    from_next = lax.broadcasted_iota(jnp.int32, (n, n), 0) < row
    for own, halo, where in ((own_s, halo_s, section), (own_o, halo_o, 1 - section)):
        for d in range(depth):
            for ri in range(2):
                merged = jnp.where(from_next, halo[ri, d], own[ri, d])
                patch[where * depth + d, ri] = pltpu.roll(merged, unroll_by, 0)

    def toeplitz(k):
        rows = jnp.broadcast_to(ring[k : k + 1, :], (n, 2 * n))
        return pltpu.roll(rows, 0, 1, stride=1, stride_axis=0)[:, :n]

    for high, low, kr, ki in ((ah, al, toeplitz(0), -toeplitz(1)), (bh, bl, toeplitz(2), toeplitz(3))):
        for r0, c0, block in ((0, 0, kr), (0, n, ki), (n, 0, -ki), (n, n, kr)):
            hi, lo = halves(block)
            high[r0 : r0 + n, c0 : c0 + n] = hi
            low[r0 : r0 + n, c0 : c0 + n] = lo

    waves[0] = probe[...]
    slices = 2 * depth

    def forward(s, _):
        pr, pi = waves[s, 0], waves[s, 1]
        o_r, o_i = patch[s, 0], patch[s, 1]
        zr, zi = sandwich(
            ah[...], al[...], pr * o_r - pi * o_i, pr * o_i + pi * o_r, bh[...], bl[...]
        )
        waves[s + 1, 0] = zr
        waves[s + 1, 1] = zi
        return 0

    lax.fori_loop(0, slices, forward, 0)
    fr, fi = sandwich(
        ch[...], cl[...], waves[slices, 0], waves[slices, 1], dh[...], dl[...]
    )
    residual = 2.0 * (fr * fr + fi * fi - intensity[section])
    xr, xi = sandwich(dh[...], dl[...], residual * fr, residual * fi, ch[...], cl[...])
    waves[slices, 0] = xr
    waves[slices, 1] = xi

    def backward(t, _):
        s = slices - 1 - t
        a_r, a_i = sandwich(
            bh[...], bl[...], waves[s + 1, 0], waves[s + 1, 1], ah[...], al[...]
        )
        w_r, w_i = waves[s, 0], waves[s, 1]
        o_r, o_i = patch[s, 0], patch[s, 1]
        patch[s, 0] = a_r * w_r + a_i * w_i
        patch[s, 1] = a_i * w_r - a_r * w_i
        waves[s, 0] = a_r * o_r + a_i * o_i
        waves[s, 1] = a_i * o_r - a_r * o_i
        return 0

    lax.fori_loop(0, slices, backward, 0)
    for out, where in ((term_s, section), (term_o, 1 - section)):
        for d in range(depth):
            for ri in range(2):
                out[ri, d] = pltpu.roll(patch[where * depth + d, ri], row, 0)


def deposit_kernel(rows, cols, own_s, own_o, rim_s, rim_o, out_r, out_i):
    n = own_s.shape[-1]
    span = n + 128
    row_index = lax.broadcasted_iota(jnp.int32, (n, n), 0)
    for ri, out in enumerate((out_r, out_i)):
        out[...] = jnp.zeros_like(out)
        for k, src in enumerate((own_s, own_o, rim_s, rim_o)):
            keep = row_index >= rows[k] if k < 2 else row_index < rows[k]
            term = jnp.where(keep, src[ri, 0], 0.0)
            base, shift = column_place(cols[k], out.shape[-1], span)
            wide = jnp.concatenate([term, jnp.zeros((n, 128), F32)], 1)
            out[0, :, pl.ds(base, span)] += pltpu.roll(wide, shift, 1)


def local(obj_real, obj_imag, probe, taps, intensity, row_off, col_off):
    n = probe.shape[-1]
    depth, tile, cols_all = obj_real.shape
    npos, nslab = lax.axis_size("pos"), lax.axis_size("slab")
    section = lax.axis_index("slab")

    def ring_pairs(step, flip):
        pairs = []
        for p in range(npos):
            for s in range(nslab):
                to = ((p + step) % npos) * nslab + (1 - s if flip else s)
                pairs.append((p * nslab + s, to))
        return pairs

    def send(x, step, flip):
        return lax.ppermute(x, ("pos", "slab"), ring_pairs(step, flip))

    order = jnp.stack([section, 1 - section])
    mine = jnp.stack([row_off, col_off])[:, order]
    before = send(mine, 1, False)
    rows = jnp.concatenate([mine[0], before[0]])
    cols = jnp.concatenate([mine[1], before[1]])

    window = jax.ShapeDtypeStruct((2, depth, n, n), F32)
    window_spec = pl.BlockSpec((2, 1, n, n), lambda d: (0, d, 0, 0))
    plane_spec = pl.BlockSpec((1, tile, cols_all), lambda d: (d, 0, 0))
    own_s, own_o, halo_s, halo_o = pl.pallas_call(
        cut_kernel,
        grid=(depth,),
        out_shape=[window] * 4,
        in_specs=[SMEM, plane_spec, plane_spec],
        out_specs=[window_spec] * 4,
        compiler_params=pltpu.CompilerParams(vmem_limit_bytes=40 * 2**20),
        name="cut",
    )(cols, obj_real, obj_imag)
    halo_s = send(halo_s, -1, False)
    halo_o = send(halo_o, -1, True)
    own_o = send(own_o, 0, True)

    half = (taps.shape[1] - 1) // 2
    gap = jnp.zeros((2, 2 * n - taps.shape[1]), F32)
    back = taps[:, ::-1]
    ring = jnp.concatenate(
        [
            jnp.concatenate([t[:, half:], gap, t[:, :half]], 1)
            for t in (taps, back)
        ],
        0,
    )
    info = jnp.stack([section, rows[0]]).astype(jnp.int32)
    square = pltpu.VMEM((2 * n, 2 * n), BF16)
    term_s, term_o = pl.pallas_call(
        wave_kernel,
        out_shape=[window] * 2,
        in_specs=[SMEM] + [VMEM] * 11,
        out_specs=[VMEM] * 2,
        scratch_shapes=[
            pltpu.VMEM((2 * depth, 2, n, n), F32),
            pltpu.VMEM((2 * depth + 1, 2, n, n), F32),
            square, square, square, square,
        ],
        compiler_params=pltpu.CompilerParams(vmem_limit_bytes=48 * 2**20),
        name="waves",
    )(info, own_s, own_o, halo_s, halo_o, probe, ring, intensity, *fourier_blocks(n))

    rim_s = send(term_s, 1, False)
    rim_o = send(term_o, 1, True)
    own_o = send(term_o, 0, True)
    return pl.pallas_call(
        deposit_kernel,
        grid=(depth,),
        out_shape=[jax.ShapeDtypeStruct(obj_real.shape, F32)] * 2,
        in_specs=[SMEM, SMEM] + [window_spec] * 4,
        out_specs=[plane_spec] * 2,
        compiler_params=pltpu.CompilerParams(vmem_limit_bytes=40 * 2**20),
        name="deposit",
    )(rows, cols, term_s, own_o, rim_s, rim_o)


def solution(mesh):
    in_specs = (
        P(("parts", "slab"), "pos", None),
        P(("parts", "slab"), "pos", None),
        P(),
        P(),
        P(("parts", "pos"), None, None),
        P(("parts", "pos")),
        P(("parts", "pos")),
    )
    out_specs = (P(("parts", "slab"), "pos", None), P(("parts", "slab"), "pos", None))
    return jax.shard_map(local, mesh=mesh, in_specs=in_specs, out_specs=out_specs, check_vma=False)
```

```python
import functools
import math

import jax
import jax.numpy as jnp
import numpy as np
from jax import lax
from jax.experimental import pallas as pl
from jax.experimental.pallas import tpu as pltpu
from jax.sharding import PartitionSpec as P

F32 = jnp.float32
BF16 = jnp.bfloat16
SMEM = pl.BlockSpec(memory_space=pltpu.SMEM)
VMEM = pl.BlockSpec(memory_space=pltpu.VMEM)


def halves(x):
    high = x.astype(BF16)
    return high, (x - high.astype(F32)).astype(BF16)


def left_mul(high, low, x):
    xh, xl = halves(x)
    left = jnp.concatenate([high, high, low], 1)
    right = jnp.concatenate([xh, xl, xh], 0)
    return jnp.dot(left, right, preferred_element_type=F32)


def right_mul(x, high, low):
    xh, xl = halves(x)
    left = jnp.concatenate([xh, xl, xh], 1)
    right = jnp.concatenate([high, high, low], 0)
    return jnp.dot(left, right, preferred_element_type=F32)


def sandwich(left_h, left_l, xr, xi, right_h, right_l):
    n = xr.shape[0]
    y = left_mul(left_h, left_l, jnp.concatenate([xr, xi], 0))
    z = right_mul(jnp.concatenate([y[:n], y[n:]], 1), right_h, right_l)
    return z[:, :n], z[:, n:]


def fourier_blocks(n):
    steps = np.arange(n)
    angle = 2.0 * math.pi / n * ((steps[:, None] * steps[None, :]) % n)
    norm = 1.0 / math.sqrt(n)
    wr, wi = np.cos(angle) * norm, -np.sin(angle) * norm
    c = np.block([[wr, -wi], [wi, wr]]).astype(np.float32)
    d = np.block([[wr, wi], [-wi, wr]]).astype(np.float32)
    out = []
    for m in (c, d):
        high = m.astype(jnp.bfloat16)
        out += [high, (m - high.astype(np.float32)).astype(jnp.bfloat16)]
    return [jnp.asarray(m) for m in out]


def column_place(col, cols_all, span):
    base = jnp.minimum(col // 128 * 128, cols_all - span)
    return pl.multiple_of(base, 128), col - base


def cut_kernel(cols, obj_r, obj_i, *rest):
    outs = rest[-cols.shape[0] :]
    n = outs[0].shape[-1]
    span = n + 128
    for k, out in enumerate(outs):
        base, shift = column_place(cols[k], obj_r.shape[-1], span)
        for ri, src in enumerate((obj_r, obj_i)):
            wide = src[0, :, pl.ds(base, span)]
            out[ri, 0] = pltpu.roll(wide, lax.rem(span - shift, span), 1)[:, :n]


def wave_kernel(phase, info, *refs):
    if phase > 0:
        refs = refs[:11] + refs[12:]

    @pl.when(info[0] == phase)
    def _():
        wave_body(info, *refs)


def wave_body(
    info, own_s, own_o, halo_s, halo_o, probe, ring, intensity, ch, cl, dh, dl,
    term_s, term_o, patch, waves, ah, al, bh, bl,
):
    n = probe.shape[-1]
    depth = own_s.shape[1]
    section, row = info[0], info[1]
    unroll_by = lax.rem(n - row, n)
    from_next = lax.broadcasted_iota(jnp.int32, (n, n), 0) < row
    for own, halo, where in ((own_s, halo_s, section), (own_o, halo_o, 1 - section)):
        for d in range(depth):
            for ri in range(2):
                merged = jnp.where(from_next, halo[ri, d], own[ri, d])
                patch[where * depth + d, ri] = pltpu.roll(merged, unroll_by, 0)

    def toeplitz(k):
        rows = jnp.broadcast_to(ring[k : k + 1, :], (n, 2 * n))
        return pltpu.roll(rows, 0, 1, stride=1, stride_axis=0)[:, :n]

    for high, low, kr, ki in ((ah, al, toeplitz(0), -toeplitz(1)), (bh, bl, toeplitz(2), toeplitz(3))):
        for r0, c0, block in ((0, 0, kr), (0, n, ki), (n, 0, -ki), (n, n, kr)):
            hi, lo = halves(block)
            high[r0 : r0 + n, c0 : c0 + n] = hi
            low[r0 : r0 + n, c0 : c0 + n] = lo

    waves[0] = probe[...]
    slices = 2 * depth

    def forward(s, _):
        pr, pi = waves[s, 0], waves[s, 1]
        o_r, o_i = patch[s, 0], patch[s, 1]
        zr, zi = sandwich(
            ah[...], al[...], pr * o_r - pi * o_i, pr * o_i + pi * o_r, bh[...], bl[...]
        )
        waves[s + 1, 0] = zr
        waves[s + 1, 1] = zi
        return 0

    lax.fori_loop(0, slices, forward, 0)
    fr, fi = sandwich(
        ch[...], cl[...], waves[slices, 0], waves[slices, 1], dh[...], dl[...]
    )
    residual = 2.0 * (fr * fr + fi * fi - intensity[section])
    xr, xi = sandwich(dh[...], dl[...], residual * fr, residual * fi, ch[...], cl[...])
    waves[slices, 0] = xr
    waves[slices, 1] = xi

    def backward(t, _):
        s = slices - 1 - t
        a_r, a_i = sandwich(
            bh[...], bl[...], waves[s + 1, 0], waves[s + 1, 1], ah[...], al[...]
        )
        w_r, w_i = waves[s, 0], waves[s, 1]
        o_r, o_i = patch[s, 0], patch[s, 1]
        patch[s, 0] = a_r * w_r + a_i * w_i
        patch[s, 1] = a_i * w_r - a_r * w_i
        waves[s, 0] = a_r * o_r + a_i * o_i
        waves[s, 1] = a_i * o_r - a_r * o_i
        return 0

    lax.fori_loop(0, slices, backward, 0)
    for out, where in ((term_s, section), (term_o, 1 - section)):
        for d in range(depth):
            for ri in range(2):
                out[ri, d] = pltpu.roll(patch[where * depth + d, ri], row, 0)


def deposit_kernel(section, rows, cols, *refs):
    pieces, (out_r, out_i) = refs[:8], refs[8:]
    n = pieces[0].shape[-1]
    span = n + 128
    row_index = lax.broadcasted_iota(jnp.int32, (n, n), 0)
    first = section[0] == 0
    for ri, out in enumerate((out_r, out_i)):
        out[...] = jnp.zeros_like(out)
        for k in range(4):
            keep = row_index >= rows[k] if k < 2 else row_index < rows[k]
            term = jnp.where(first, pieces[2 * k][ri, 0], pieces[2 * k + 1][ri, 0])
            term = jnp.where(keep, term, 0.0)
            base, shift = column_place(cols[k], out.shape[-1], span)
            wide = jnp.concatenate([term, jnp.zeros((n, 128), F32)], 1)
            out[0, :, pl.ds(base, span)] += pltpu.roll(wide, shift, 1)


def local(obj_real, obj_imag, probe, taps, intensity, row_off, col_off):
    n = probe.shape[-1]
    depth, tile, cols_all = obj_real.shape
    npos, nslab = lax.axis_size("pos"), lax.axis_size("slab")
    section = lax.axis_index("slab")

    def send(x, step, routes):
        pairs = [
            (p * nslab + src, ((p + step) % npos) * nslab + dst)
            for p in range(npos)
            for src, dst in routes
        ]
        return lax.ppermute(x, ("pos", "slab"), pairs)

    given = jnp.stack([row_off, col_off])
    tile_before = send(given, 1, ((0, 0), (1, 1)))
    order = jnp.stack([section, 1 - section])
    mine, before = given[:, order], tile_before[:, order]
    rows = jnp.concatenate([mine[0], before[0]])
    cols = jnp.concatenate([mine[1], before[1]])

    window = jax.ShapeDtypeStruct((2, depth, n, n), F32)
    window_spec = pl.BlockSpec((2, 1, n, n), lambda d: (0, d, 0, 0))
    plane_spec = pl.BlockSpec((1, tile, cols_all), lambda d: (d, 0, 0))
    anywhere = pl.BlockSpec(memory_space=pl.ANY)

    def cut(places, *after):
        count = places.shape[0]
        return pl.pallas_call(
            cut_kernel,
            grid=(depth,),
            out_shape=[window] * count,
            in_specs=[SMEM, plane_spec, plane_spec] + [anywhere] * len(after),
            out_specs=[window_spec] * count,
            compiler_params=pltpu.CompilerParams(vmem_limit_bytes=40 * 2**20),
            cost_estimate=pl.CostEstimate(flops=0, bytes_accessed=8 * 2**20, transcendentals=0),
            name="cut",
        )(places, obj_real, obj_imag, *after)

    (first_halo,) = cut(tile_before[1, :1])
    halos = [[send(first_halo, -1, ((0, 0),)), send(first_halo, -1, ((1, 0),))]]
    second_halo, own_s, own_o = cut(
        jnp.concatenate([tile_before[1, 1:], mine[1]]), first_halo
    )
    halos.append([send(second_halo, -1, ((1, 1),)), send(second_halo, -1, ((0, 1),))])
    own_o = send(own_o, 0, ((0, 1), (1, 0)))

    half = (taps.shape[1] - 1) // 2
    gap = jnp.zeros((2, 2 * n - taps.shape[1]), F32)
    back = taps[:, ::-1]
    ring = jnp.concatenate(
        [
            jnp.concatenate([t[:, half:], gap, t[:, :half]], 1)
            for t in (taps, back)
        ],
        0,
    )
    info = jnp.stack([section, rows[0]]).astype(jnp.int32)
    square = pltpu.VMEM((2 * n, 2 * n), BF16)
    constants = fourier_blocks(n)

    def waves(phase, *after):
        return pl.pallas_call(
            functools.partial(wave_kernel, phase),
            out_shape=[window] * 2,
            in_specs=[SMEM] + [VMEM] * 11 + [anywhere] * len(after),
            out_specs=[VMEM] * 2,
            scratch_shapes=[
                pltpu.VMEM((2 * depth, 2, n, n), F32),
                pltpu.VMEM((2 * depth + 1, 2, n, n), F32),
                square, square, square, square,
            ],
            compiler_params=pltpu.CompilerParams(vmem_limit_bytes=48 * 2**20),
            cost_estimate=pl.CostEstimate(
                flops=(8 * depth + 4) * 24 * n**3, bytes_accessed=2**23, transcendentals=0
            ),
            name="waves",
        )(info, own_s, own_o, *halos[phase], probe, ring, intensity, *constants, *after)

    terms = [waves(0)]
    terms.append(waves(1, terms[0][0]))
    pieces = [[], [], [], []]
    for k, (same, other) in enumerate(terms):
        pieces[0].append(same)
        pieces[1].append(send(other, 0, ((k, 1 - k),)))
        pieces[2].append(send(same, 1, ((k, k),)))
        pieces[3].append(send(other, 1, ((k, 1 - k),)))
    for k in (1, 3):
        pieces[k].reverse()
    return pl.pallas_call(
        deposit_kernel,
        grid=(depth,),
        out_shape=[jax.ShapeDtypeStruct(obj_real.shape, F32)] * 2,
        in_specs=[SMEM] * 3 + [window_spec] * 8,
        out_specs=[plane_spec] * 2,
        compiler_params=pltpu.CompilerParams(vmem_limit_bytes=40 * 2**20),
        name="deposit",
    )(info[:1], rows, cols, *pieces[0], *pieces[1], *pieces[2], *pieces[3])


def solution(mesh):
    in_specs = (
        P(("parts", "slab"), "pos", None),
        P(("parts", "slab"), "pos", None),
        P(),
        P(),
        P(("parts", "pos"), None, None),
        P(("parts", "pos")),
        P(("parts", "pos")),
    )
    out_specs = (P(("parts", "slab"), "pos", None), P(("parts", "slab"), "pos", None))
    return jax.shard_map(local, mesh=mesh, in_specs=in_specs, out_specs=out_specs, check_vma=False)
```

```python
import functools
import math

import jax
import jax.numpy as jnp
import numpy as np
from jax import lax
from jax.experimental import pallas as pl
from jax.experimental.pallas import tpu as pltpu
from jax.sharding import PartitionSpec as P

F32 = jnp.float32
BF16 = jnp.bfloat16
SMEM = pl.BlockSpec(memory_space=pltpu.SMEM)
VMEM = pl.BlockSpec(memory_space=pltpu.VMEM)


def halves(x):
    high = x.astype(BF16)
    return high, (x - high.astype(F32)).astype(BF16)


def left_mul(high, low, x):
    xh, xl = halves(x)
    left = jnp.concatenate([high, high, low], 1)
    right = jnp.concatenate([xh, xl, xh], 0)
    return jnp.dot(left, right, preferred_element_type=F32)


def right_mul(x, high, low):
    xh, xl = halves(x)
    left = jnp.concatenate([xh, xl, xh], 1)
    right = jnp.concatenate([high, high, low], 0)
    return jnp.dot(left, right, preferred_element_type=F32)


def sandwich(left_h, left_l, xr, xi, right_h, right_l):
    n = xr.shape[0]
    y = left_mul(left_h, left_l, jnp.concatenate([xr, xi], 0))
    z = right_mul(jnp.concatenate([y[:n], y[n:]], 1), right_h, right_l)
    return z[:, :n], z[:, n:]


def fourier_blocks(n):
    steps = np.arange(n)
    angle = 2.0 * math.pi / n * ((steps[:, None] * steps[None, :]) % n)
    norm = 1.0 / math.sqrt(n)
    wr, wi = np.cos(angle) * norm, -np.sin(angle) * norm
    c = np.block([[wr, -wi], [wi, wr]]).astype(np.float32)
    d = np.block([[wr, wi], [-wi, wr]]).astype(np.float32)
    out = []
    for m in (c, d):
        high = m.astype(jnp.bfloat16)
        out += [high, (m - high.astype(np.float32)).astype(jnp.bfloat16)]
    return jnp.asarray(np.stack(out))


def column_place(col, cols_all, span):
    base = jnp.minimum(col // 128 * 128, cols_all - span)
    return pl.multiple_of(base, 128), col - base


def cut_kernel(cols, obj_r, obj_i, *rest):
    outs = rest[-cols.shape[0] :]
    n = outs[0].shape[-1]
    span = n + 128
    for k, out in enumerate(outs):
        base, shift = column_place(cols[k], obj_r.shape[-1], span)
        for ri, src in enumerate((obj_r, obj_i)):
            wide = src[0, :, pl.ds(base, span)]
            out[ri, 0] = pltpu.roll(wide, lax.rem(span - shift, span), 1)[:, :n]


def band_kernel(ring, out):
    n = out.shape[-1] // 2

    def toeplitz(k):
        rows = jnp.broadcast_to(ring[k : k + 1, :], (n, 2 * n))
        return pltpu.roll(rows, 0, 1, stride=1, stride_axis=0)[:, :n]

    for k, kr, ki in ((0, toeplitz(0), -toeplitz(1)), (2, toeplitz(2), toeplitz(3))):
        for r0, c0, block in ((0, 0, kr), (0, n, ki), (n, 0, -ki), (n, n, kr)):
            hi, lo = halves(block)
            out[k, r0 : r0 + n, c0 : c0 + n] = hi
            out[k + 1, r0 : r0 + n, c0 : c0 + n] = lo


def wave_kernel(phase, info, *refs):
    if phase > 0:
        refs = refs[:8] + refs[9:]

    @pl.when(info[0] == phase)
    def _():
        wave_body(info, *refs)


def wave_body(
    info, own_s, own_o, halo_s, halo_o, probe, intensity, bands, fourier, term_s, term_o,
    own, halo, patch, waves, measured, band, dft, in_sem, out_sem, side_sem,
):
    n = probe.shape[-1]
    depth = own_s.shape[1]
    slices = 2 * depth
    section, row = info[0], info[1]
    unroll_by = lax.rem(n - row, n)
    from_next = lax.broadcasted_iota(jnp.int32, (n, n), 0) < row

    lead = pltpu.make_async_copy(probe, waves.at[0], side_sem.at[0])
    band_in = pltpu.make_async_copy(bands, band, side_sem.at[1])
    dft_in = pltpu.make_async_copy(fourier, dft, side_sem.at[2])
    measured_in = pltpu.make_async_copy(intensity.at[section], measured, side_sem.at[3])

    def incoming(source, target, kind, slot, d):
        return pltpu.make_async_copy(source.at[:, d], target.at[slot], in_sem.at[kind, slot])

    lead.start()
    band_in.start()
    for d in range(depth):
        for o, h, where in ((own_s, halo_s, section), (own_o, halo_o, 1 - section)):
            incoming(o, own, 0, where * depth + d, d).start()
            incoming(h, halo, 1, where * depth + d, d).start()
    dft_in.start()
    measured_in.start()
    lead.wait()
    band_in.wait()

    def forward(s, _):
        incoming(own_s, own, 0, s, 0).wait()
        incoming(halo_s, halo, 1, s, 0).wait()
        for ri in range(2):
            merged = jnp.where(from_next, halo[s, ri], own[s, ri])
            patch[s, ri] = pltpu.roll(merged, unroll_by, 0)
        pr, pi = waves[s, 0], waves[s, 1]
        o_r, o_i = patch[s, 0], patch[s, 1]
        zr, zi = sandwich(
            band[0], band[1], pr * o_r - pi * o_i, pr * o_i + pi * o_r, band[2], band[3]
        )
        waves[s + 1, 0] = zr
        waves[s + 1, 1] = zi
        return 0

    lax.fori_loop(0, slices, forward, 0)
    dft_in.wait()
    measured_in.wait()
    fr, fi = sandwich(dft[0], dft[1], waves[slices, 0], waves[slices, 1], dft[2], dft[3])
    residual = 2.0 * (fr * fr + fi * fi - measured[...])
    xr, xi = sandwich(dft[2], dft[3], residual * fr, residual * fi, dft[0], dft[1])
    waves[slices, 0] = xr
    waves[slices, 1] = xi

    def outgoing(slot, out, d):
        return pltpu.make_async_copy(own.at[slot], out.at[:, d], out_sem.at[slot])

    def backward(t, _):
        s = slices - 1 - t
        a_r, a_i = sandwich(
            band[2], band[3], waves[s + 1, 0], waves[s + 1, 1], band[0], band[1]
        )
        w_r, w_i = waves[s, 0], waves[s, 1]
        o_r, o_i = patch[s, 0], patch[s, 1]
        own[s, 0] = pltpu.roll(a_r * w_r + a_i * w_i, row, 0)
        own[s, 1] = pltpu.roll(a_i * w_r - a_r * w_i, row, 0)
        waves[s, 0] = a_r * o_r + a_i * o_i
        waves[s, 1] = a_i * o_r - a_r * o_i
        group = s // depth

        @pl.when(group == section)
        def _():
            outgoing(s, term_s, s - group * depth).start()

        @pl.when(group != section)
        def _():
            outgoing(s, term_o, s - group * depth).start()

        return 0

    lax.fori_loop(0, slices, backward, 0)
    for s in range(slices):
        outgoing(s, term_s, 0).wait()


def deposit_kernel(section, rows, cols, *refs):
    pieces, (out_r, out_i) = refs[:8], refs[8:]
    n = pieces[0].shape[-1]
    span = n + 128
    row_index = lax.broadcasted_iota(jnp.int32, (n, n), 0)
    first = section[0] == 0
    for ri, out in enumerate((out_r, out_i)):
        out[...] = jnp.zeros_like(out)
        for k in range(4):
            keep = row_index >= rows[k] if k < 2 else row_index < rows[k]
            term = jnp.where(first, pieces[2 * k][ri, 0], pieces[2 * k + 1][ri, 0])
            term = jnp.where(keep, term, 0.0)
            base, shift = column_place(cols[k], out.shape[-1], span)
            wide = jnp.concatenate([term, jnp.zeros((n, 128), F32)], 1)
            out[0, :, pl.ds(base, span)] += pltpu.roll(wide, shift, 1)


def local(obj_real, obj_imag, probe, taps, intensity, row_off, col_off):
    n = probe.shape[-1]
    depth, tile, cols_all = obj_real.shape
    npos, nslab = lax.axis_size("pos"), lax.axis_size("slab")
    section = lax.axis_index("slab")

    def send(x, step, routes):
        pairs = [
            (p * nslab + src, ((p + step) % npos) * nslab + dst)
            for p in range(npos)
            for src, dst in routes
        ]
        return lax.ppermute(x, ("pos", "slab"), pairs)

    given = jnp.stack([row_off, col_off])
    tile_before = send(given, 1, ((0, 0), (1, 1)))
    order = jnp.stack([section, 1 - section])
    mine, before = given[:, order], tile_before[:, order]
    rows = jnp.concatenate([mine[0], before[0]])
    cols = jnp.concatenate([mine[1], before[1]])

    window = jax.ShapeDtypeStruct((2, depth, n, n), F32)
    window_spec = pl.BlockSpec((2, 1, n, n), lambda d: (0, d, 0, 0))
    plane_spec = pl.BlockSpec((1, tile, cols_all), lambda d: (d, 0, 0))
    anywhere = pl.BlockSpec(memory_space=pl.ANY)

    def cut(places, *after):
        count = places.shape[0]
        return pl.pallas_call(
            cut_kernel,
            grid=(depth,),
            out_shape=[window] * count,
            in_specs=[SMEM, plane_spec, plane_spec] + [anywhere] * len(after),
            out_specs=[window_spec] * count,
            compiler_params=pltpu.CompilerParams(vmem_limit_bytes=40 * 2**20),
            cost_estimate=pl.CostEstimate(flops=0, bytes_accessed=8 * 2**20, transcendentals=0),
            name="cut",
        )(places, obj_real, obj_imag, *after)

    (first_halo,) = cut(tile_before[1, :1])
    halos = [[send(first_halo, -1, ((0, 0),)), send(first_halo, -1, ((1, 0),))]]
    second_halo, own_s, own_o = cut(
        jnp.concatenate([tile_before[1, 1:], mine[1]]), first_halo
    )
    halos.append([send(second_halo, -1, ((1, 1),)), send(second_halo, -1, ((0, 1),))])
    own_o = send(own_o, 0, ((0, 1), (1, 0)))

    half = (taps.shape[1] - 1) // 2
    gap = jnp.zeros((2, 2 * n - taps.shape[1]), F32)
    back = taps[:, ::-1]
    ring = jnp.concatenate(
        [
            jnp.concatenate([t[:, half:], gap, t[:, :half]], 1)
            for t in (taps, back)
        ],
        0,
    )
    info = jnp.stack([section, rows[0]]).astype(jnp.int32)
    fourier = fourier_blocks(n)
    bands = pl.pallas_call(
        band_kernel,
        out_shape=jax.ShapeDtypeStruct((4, 2 * n, 2 * n), BF16),
        in_specs=[VMEM],
        out_specs=VMEM,
        compiler_params=pltpu.CompilerParams(vmem_limit_bytes=40 * 2**20),
        name="band",
    )(ring)

    def waves(phase, *after):
        stack = pltpu.VMEM((2 * depth, 2, n, n), F32)
        matrices = pltpu.VMEM((4, 2 * n, 2 * n), BF16)
        return pl.pallas_call(
            functools.partial(wave_kernel, phase),
            out_shape=[window] * 2,
            in_specs=[SMEM] + [anywhere] * (8 + len(after)),
            out_specs=[anywhere] * 2,
            scratch_shapes=[
                stack, stack, stack,
                pltpu.VMEM((2 * depth + 1, 2, n, n), F32),
                pltpu.VMEM((n, n), F32),
                matrices, matrices,
                pltpu.SemaphoreType.DMA((2, 2 * depth)),
                pltpu.SemaphoreType.DMA((2 * depth,)),
                pltpu.SemaphoreType.DMA((4,)),
            ],
            compiler_params=pltpu.CompilerParams(vmem_limit_bytes=44 * 2**20),
            cost_estimate=pl.CostEstimate(
                flops=(8 * depth + 4) * 24 * n**3, bytes_accessed=2**23, transcendentals=0
            ),
            name="waves",
        )(info, own_s, own_o, *halos[phase], probe, intensity, bands, fourier, *after)

    terms = [waves(0)]
    swapped = send(terms[0][1], 0, ((0, 1),))
    terms.append(waves(1, swapped))
    pieces = [[], [], [], []]
    for k, (same, other) in enumerate(terms):
        pieces[0].append(same)
        pieces[1].append(swapped if k == 0 else send(other, 0, ((k, 1 - k),)))
        pieces[2].append(send(same, 1, ((k, k),)))
        pieces[3].append(send(other, 1, ((k, 1 - k),)))
    for k in (1, 3):
        pieces[k].reverse()
    return pl.pallas_call(
        deposit_kernel,
        grid=(depth,),
        out_shape=[jax.ShapeDtypeStruct(obj_real.shape, F32)] * 2,
        in_specs=[SMEM] * 3 + [window_spec] * 8,
        out_specs=[plane_spec] * 2,
        compiler_params=pltpu.CompilerParams(vmem_limit_bytes=40 * 2**20),
        name="deposit",
    )(info[:1], rows, cols, *pieces[0], *pieces[1], *pieces[2], *pieces[3])


def solution(mesh):
    in_specs = (
        P(("parts", "slab"), "pos", None),
        P(("parts", "slab"), "pos", None),
        P(),
        P(),
        P(("parts", "pos"), None, None),
        P(("parts", "pos")),
        P(("parts", "pos")),
    )
    out_specs = (P(("parts", "slab"), "pos", None), P(("parts", "slab"), "pos", None))
    return jax.shard_map(local, mesh=mesh, in_specs=in_specs, out_specs=out_specs, check_vma=False)
```

```python
import functools
import math

import jax
import jax.numpy as jnp
import numpy as np
from jax import lax
from jax.experimental import pallas as pl
from jax.experimental.pallas import tpu as pltpu
from jax.sharding import PartitionSpec as P

F32 = jnp.float32
BF16 = jnp.bfloat16
SMEM = pl.BlockSpec(memory_space=pltpu.SMEM)
VMEM = pl.BlockSpec(memory_space=pltpu.VMEM)


def halves(x):
    high = x.astype(BF16)
    return high, (x - high.astype(F32)).astype(BF16)


def left_mul(high, low, x):
    xh, xl = halves(x)
    left = jnp.concatenate([high, high, low], 1)
    right = jnp.concatenate([xh, xl, xh], 0)
    return jnp.dot(left, right, preferred_element_type=F32)


def right_mul(x, high, low):
    xh, xl = halves(x)
    left = jnp.concatenate([xh, xl, xh], 1)
    right = jnp.concatenate([high, high, low], 0)
    return jnp.dot(left, right, preferred_element_type=F32)


def sandwich(left_h, left_l, xr, xi, right_h, right_l):
    n = xr.shape[0]
    y = left_mul(left_h, left_l, jnp.concatenate([xr, xi], 0))
    z = right_mul(jnp.concatenate([y[:n], y[n:]], 1), right_h, right_l)
    return z[:, :n], z[:, n:]


def fourier_blocks(n):
    steps = np.arange(n)
    angle = 2.0 * math.pi / n * ((steps[:, None] * steps[None, :]) % n)
    norm = 1.0 / math.sqrt(n)
    wr, wi = np.cos(angle) * norm, -np.sin(angle) * norm
    c = np.block([[wr, -wi], [wi, wr]]).astype(np.float32)
    d = np.block([[wr, wi], [-wi, wr]]).astype(np.float32)
    out = []
    for m in (c, d):
        high = m.astype(jnp.bfloat16)
        out += [high, (m - high.astype(np.float32)).astype(jnp.bfloat16)]
    return jnp.asarray(np.stack(out))


def column_place(col, cols_all, span):
    base = jnp.minimum(col // 128 * 128, cols_all - span)
    return pl.multiple_of(base, 128), col - base


def cut_kernel(cols, obj_r, obj_i, *rest):
    outs = rest[-cols.shape[0] :]
    n = outs[0].shape[-1]
    span = n + 128
    for k, out in enumerate(outs):
        base, shift = column_place(cols[k], obj_r.shape[-1], span)
        for ri, src in enumerate((obj_r, obj_i)):
            wide = src[0, :, pl.ds(base, span)]
            out[ri, 0] = pltpu.roll(wide, lax.rem(span - shift, span), 1)[:, :n]


def band_kernel(ring, out):
    n = out.shape[-1] // 2

    def toeplitz(k):
        rows = jnp.broadcast_to(ring[k : k + 1, :], (n, 2 * n))
        return pltpu.roll(rows, 0, 1, stride=1, stride_axis=0)[:, :n]

    for k, kr, ki in ((0, toeplitz(0), -toeplitz(1)), (2, toeplitz(2), toeplitz(3))):
        for r0, c0, block in ((0, 0, kr), (0, n, ki), (n, 0, -ki), (n, n, kr)):
            hi, lo = halves(block)
            out[k, r0 : r0 + n, c0 : c0 + n] = hi
            out[k + 1, r0 : r0 + n, c0 : c0 + n] = lo


def wave_kernel(phase, info, *refs):
    if phase > 0:
        refs = refs[:8] + refs[9:]

    @pl.when(info[0] == phase)
    def _():
        wave_body(info, *refs)


def wave_body(
    info, own_s, own_o, halo_s, halo_o, probe, intensity, bands, fourier, term_s, term_o,
    own, halo, patch, waves, measured, band, dft, in_sem, out_sem, side_sem,
):
    n = probe.shape[-1]
    depth = own_s.shape[1]
    slices = 2 * depth
    section, row = info[0], info[1]
    unroll_by = lax.rem(n - row, n)
    from_next = lax.broadcasted_iota(jnp.int32, (n, n), 0) < row

    lead = pltpu.make_async_copy(probe, waves.at[0], side_sem.at[0])
    band_in = pltpu.make_async_copy(bands, band, side_sem.at[1])
    dft_in = pltpu.make_async_copy(fourier, dft, side_sem.at[2])
    measured_in = pltpu.make_async_copy(intensity.at[section], measured, side_sem.at[3])

    def incoming(source, target, kind, slot, d):
        return pltpu.make_async_copy(source.at[:, d], target.at[slot], in_sem.at[kind, slot])

    lead.start()
    band_in.start()
    for d in range(depth):
        for o, h, where in ((own_s, halo_s, section), (own_o, halo_o, 1 - section)):
            incoming(o, own, 0, where * depth + d, d).start()
            incoming(h, halo, 1, where * depth + d, d).start()
    dft_in.start()
    measured_in.start()
    lead.wait()
    band_in.wait()

    def forward(s, _):
        incoming(own_s, own, 0, s, 0).wait()
        incoming(halo_s, halo, 1, s, 0).wait()
        for ri in range(2):
            merged = jnp.where(from_next, halo[s, ri], own[s, ri])
            patch[s, ri] = pltpu.roll(merged, unroll_by, 0)
        pr, pi = waves[s, 0], waves[s, 1]
        o_r, o_i = patch[s, 0], patch[s, 1]
        zr, zi = sandwich(
            band[0], band[1], pr * o_r - pi * o_i, pr * o_i + pi * o_r, band[2], band[3]
        )
        waves[s + 1, 0] = zr
        waves[s + 1, 1] = zi
        return 0

    lax.fori_loop(0, slices, forward, 0)
    dft_in.wait()
    measured_in.wait()
    fr, fi = sandwich(dft[0], dft[1], waves[slices, 0], waves[slices, 1], dft[2], dft[3])
    residual = 2.0 * (fr * fr + fi * fi - measured[...])
    xr, xi = sandwich(dft[2], dft[3], residual * fr, residual * fi, dft[0], dft[1])
    waves[slices, 0] = xr
    waves[slices, 1] = xi

    def outgoing(slot, out, d):
        return pltpu.make_async_copy(own.at[slot], out.at[:, d], out_sem.at[slot])

    def backward(t, _):
        s = slices - 1 - t
        a_r, a_i = sandwich(
            band[2], band[3], waves[s + 1, 0], waves[s + 1, 1], band[0], band[1]
        )
        w_r, w_i = waves[s, 0], waves[s, 1]
        o_r, o_i = patch[s, 0], patch[s, 1]
        own[s, 0] = pltpu.roll(a_r * w_r + a_i * w_i, row, 0)
        own[s, 1] = pltpu.roll(a_i * w_r - a_r * w_i, row, 0)
        waves[s, 0] = a_r * o_r + a_i * o_i
        waves[s, 1] = a_i * o_r - a_r * o_i
        group = s // depth

        @pl.when(group == section)
        def _():
            outgoing(s, term_s, s - group * depth).start()

        @pl.when(group != section)
        def _():
            outgoing(s, term_o, s - group * depth).start()

        return 0

    lax.fori_loop(0, slices, backward, 0)
    for s in range(slices):
        outgoing(s, term_s, 0).wait()


def deposit_kernel(section, rows, cols, *refs):
    pieces, (out_r, out_i) = refs[:8], refs[8:]
    n = pieces[0].shape[-1]
    span = n + 128
    row_index = lax.broadcasted_iota(jnp.int32, (n, n), 0)
    first = section[0] == 0
    for ri, out in enumerate((out_r, out_i)):
        out[...] = jnp.zeros_like(out)
        for k in range(4):
            keep = row_index >= rows[k] if k < 2 else row_index < rows[k]
            term = jnp.where(first, pieces[2 * k][ri, 0], pieces[2 * k + 1][ri, 0])
            term = jnp.where(keep, term, 0.0)
            base, shift = column_place(cols[k], out.shape[-1], span)
            wide = jnp.concatenate([term, jnp.zeros((n, 128), F32)], 1)
            out[0, :, pl.ds(base, span)] += pltpu.roll(wide, shift, 1)


def local(obj_real, obj_imag, probe, taps, intensity, row_off, col_off):
    n = probe.shape[-1]
    depth, tile, cols_all = obj_real.shape
    npos, nslab = lax.axis_size("pos"), lax.axis_size("slab")
    section = lax.axis_index("slab")

    def send(x, step, routes):
        pairs = [
            (p * nslab + src, ((p + step) % npos) * nslab + dst)
            for p in range(npos)
            for src, dst in routes
        ]
        return lax.ppermute(x, ("pos", "slab"), pairs)

    given = jnp.stack([row_off, col_off])
    tile_before = send(given, 1, ((0, 0), (1, 1)))
    order = jnp.stack([section, 1 - section])
    mine, before = given[:, order], tile_before[:, order]
    rows = jnp.concatenate([mine[0], before[0]])
    cols = jnp.concatenate([mine[1], before[1]])

    window = jax.ShapeDtypeStruct((2, depth, n, n), F32)
    window_spec = pl.BlockSpec((2, 1, n, n), lambda d: (0, d, 0, 0))
    plane_spec = pl.BlockSpec((1, tile, cols_all), lambda d: (d, 0, 0))
    anywhere = pl.BlockSpec(memory_space=pl.ANY)

    def cut(places, *after):
        count = places.shape[0]
        return pl.pallas_call(
            cut_kernel,
            grid=(depth,),
            out_shape=[window] * count,
            in_specs=[SMEM, plane_spec, plane_spec] + [anywhere] * len(after),
            out_specs=[window_spec] * count,
            compiler_params=pltpu.CompilerParams(vmem_limit_bytes=40 * 2**20),
            cost_estimate=pl.CostEstimate(flops=0, bytes_accessed=8 * 2**20, transcendentals=0),
            name="cut",
        )(places, obj_real, obj_imag, *after)

    (first_halo,) = cut(tile_before[1, :1])
    halos = [[send(first_halo, -1, ((0, 0),)), send(first_halo, -1, ((1, 0),))]]
    second_halo, own_s, own_o = cut(
        jnp.concatenate([tile_before[1, 1:], mine[1]]), first_halo
    )
    halos.append([send(second_halo, -1, ((1, 1),)), send(second_halo, -1, ((0, 1),))])
    own_o = send(own_o, 0, ((0, 1), (1, 0)))

    half = (taps.shape[1] - 1) // 2
    gap = jnp.zeros((2, 2 * n - taps.shape[1]), F32)
    back = taps[:, ::-1]
    ring = jnp.concatenate(
        [
            jnp.concatenate([t[:, half:], gap, t[:, :half]], 1)
            for t in (taps, back)
        ],
        0,
    )
    info = jnp.stack([section, rows[0]]).astype(jnp.int32)
    fourier = fourier_blocks(n)
    bands = pl.pallas_call(
        band_kernel,
        out_shape=jax.ShapeDtypeStruct((4, 2 * n, 2 * n), BF16),
        in_specs=[VMEM],
        out_specs=VMEM,
        compiler_params=pltpu.CompilerParams(vmem_limit_bytes=40 * 2**20),
        name="band",
    )(ring)

    def waves(phase, *after):
        stack = pltpu.VMEM((2 * depth, 2, n, n), F32)
        matrices = pltpu.VMEM((4, 2 * n, 2 * n), BF16)
        return pl.pallas_call(
            functools.partial(wave_kernel, phase),
            out_shape=[window] * 2,
            in_specs=[SMEM] + [anywhere] * (8 + len(after)),
            out_specs=[anywhere] * 2,
            scratch_shapes=[
                stack, stack, stack,
                pltpu.VMEM((2 * depth + 1, 2, n, n), F32),
                pltpu.VMEM((n, n), F32),
                matrices, matrices,
                pltpu.SemaphoreType.DMA((2, 2 * depth)),
                pltpu.SemaphoreType.DMA((2 * depth,)),
                pltpu.SemaphoreType.DMA((4,)),
            ],
            compiler_params=pltpu.CompilerParams(vmem_limit_bytes=48 * 2**20),
            cost_estimate=pl.CostEstimate(
                flops=(8 * depth + 4) * 24 * n**3, bytes_accessed=2**23, transcendentals=0
            ),
            name="waves",
        )(info, own_s, own_o, *halos[phase], probe, intensity, bands, fourier, *after)

    terms = [waves(0)]
    early = send(terms[0][0], 1, ((0, 0),))
    terms.append(waves(1, early))
    pieces = [[], [], [], []]
    for k, (same, other) in enumerate(terms):
        pieces[0].append(same)
        pieces[1].append(send(other, 0, ((k, 1 - k),)))
        pieces[2].append(early if k == 0 else send(same, 1, ((k, k),)))
        pieces[3].append(send(other, 1, ((k, 1 - k),)))
    for k in (1, 3):
        pieces[k].reverse()
    return pl.pallas_call(
        deposit_kernel,
        grid=(depth,),
        out_shape=[jax.ShapeDtypeStruct(obj_real.shape, F32)] * 2,
        in_specs=[SMEM] * 3 + [window_spec] * 8,
        out_specs=[plane_spec] * 2,
        compiler_params=pltpu.CompilerParams(vmem_limit_bytes=40 * 2**20),
        name="deposit",
    )(info[:1], rows, cols, *pieces[0], *pieces[1], *pieces[2], *pieces[3])


def solution(mesh):
    in_specs = (
        P(("parts", "slab"), "pos", None),
        P(("parts", "slab"), "pos", None),
        P(),
        P(),
        P(("parts", "pos"), None, None),
        P(("parts", "pos")),
        P(("parts", "pos")),
    )
    out_specs = (P(("parts", "slab"), "pos", None), P(("parts", "slab"), "pos", None))
    return jax.shard_map(local, mesh=mesh, in_specs=in_specs, out_specs=out_specs, check_vma=False)
```

```python
import functools
import math

import jax
import jax.numpy as jnp
import numpy as np
from jax import lax
from jax.experimental import pallas as pl
from jax.experimental.pallas import tpu as pltpu
from jax.sharding import PartitionSpec as P

F32 = jnp.float32
BF16 = jnp.bfloat16
SMEM = pl.BlockSpec(memory_space=pltpu.SMEM)
VMEM = pl.BlockSpec(memory_space=pltpu.VMEM)


def halves(x):
    high = x.astype(BF16)
    return high, (x - high.astype(F32)).astype(BF16)


def left_mul(high, low, x):
    xh, xl = halves(x)
    left = jnp.concatenate([high, high, low], 1)
    right = jnp.concatenate([xh, xl, xh], 0)
    return jnp.dot(left, right, preferred_element_type=F32)


def right_mul(x, high, low):
    xh, xl = halves(x)
    left = jnp.concatenate([xh, xl, xh], 1)
    right = jnp.concatenate([high, high, low], 0)
    return jnp.dot(left, right, preferred_element_type=F32)


def sandwich(left_h, left_l, xr, xi, right_h, right_l):
    n = xr.shape[0]
    y = left_mul(left_h, left_l, jnp.concatenate([xr, xi], 0))
    z = right_mul(jnp.concatenate([y[:n], y[n:]], 1), right_h, right_l)
    return z[:, :n], z[:, n:]


def fourier_blocks(n):
    steps = np.arange(n)
    angle = 2.0 * math.pi / n * ((steps[:, None] * steps[None, :]) % n)
    norm = 1.0 / math.sqrt(n)
    wr, wi = np.cos(angle) * norm, -np.sin(angle) * norm
    c = np.block([[wr, -wi], [wi, wr]]).astype(np.float32)
    d = np.block([[wr, wi], [-wi, wr]]).astype(np.float32)
    out = []
    for m in (c, d):
        high = m.astype(jnp.bfloat16)
        out += [high, (m - high.astype(np.float32)).astype(jnp.bfloat16)]
    return [jnp.asarray(m) for m in out]


def column_place(col, cols_all, span):
    base = jnp.minimum(col // 128 * 128, cols_all - span)
    return pl.multiple_of(base, 128), col - base


def cut_kernel(cols, obj_r, obj_i, *rest):
    outs = rest[-cols.shape[0] :]
    n = outs[0].shape[-1]
    span = n + 128
    for k, out in enumerate(outs):
        base, shift = column_place(cols[k], obj_r.shape[-1], span)
        for ri, src in enumerate((obj_r, obj_i)):
            wide = src[0, :, pl.ds(base, span)]
            out[ri, 0] = pltpu.roll(wide, lax.rem(span - shift, span), 1)[:, :n]


def band_kernel(ring, out):
    n = out.shape[-1] // 2

    def toeplitz(k):
        rows = jnp.broadcast_to(ring[k : k + 1, :], (n, 2 * n))
        return pltpu.roll(rows, 0, 1, stride=1, stride_axis=0)[:, :n]

    for k, kr, ki in ((0, toeplitz(0), -toeplitz(1)), (2, toeplitz(2), toeplitz(3))):
        for r0, c0, block in ((0, 0, kr), (0, n, ki), (n, 0, -ki), (n, n, kr)):
            hi, lo = halves(block)
            out[k, r0 : r0 + n, c0 : c0 + n] = hi
            out[k + 1, r0 : r0 + n, c0 : c0 + n] = lo


def wave_kernel(phase, info, *refs):
    if phase > 0:
        refs = refs[:11] + refs[12:]

    @pl.when(info[0] == phase)
    def _():
        wave_body(info, *refs)


def wave_body(
    info, own_s, own_o, halo_s, halo_o, probe, bands, intensity, ch, cl, dh, dl,
    term_s, term_o, patch, waves,
):
    n = probe.shape[-1]
    depth = own_s.shape[1]
    section, row = info[0], info[1]
    unroll_by = lax.rem(n - row, n)
    from_next = lax.broadcasted_iota(jnp.int32, (n, n), 0) < row
    for own, halo, where in ((own_s, halo_s, section), (own_o, halo_o, 1 - section)):
        for d in range(depth):
            for ri in range(2):
                merged = jnp.where(from_next, halo[ri, d], own[ri, d])
                patch[where * depth + d, ri] = pltpu.roll(merged, unroll_by, 0)

    ah, al, bh, bl = (bands.at[k] for k in range(4))
    waves[0] = probe[...]
    slices = 2 * depth

    def forward(s, _):
        pr, pi = waves[s, 0], waves[s, 1]
        o_r, o_i = patch[s, 0], patch[s, 1]
        zr, zi = sandwich(
            ah[...], al[...], pr * o_r - pi * o_i, pr * o_i + pi * o_r, bh[...], bl[...]
        )
        waves[s + 1, 0] = zr
        waves[s + 1, 1] = zi
        return 0

    lax.fori_loop(0, slices, forward, 0)
    fr, fi = sandwich(
        ch[...], cl[...], waves[slices, 0], waves[slices, 1], dh[...], dl[...]
    )
    residual = 2.0 * (fr * fr + fi * fi - intensity[section])
    xr, xi = sandwich(dh[...], dl[...], residual * fr, residual * fi, ch[...], cl[...])
    waves[slices, 0] = xr
    waves[slices, 1] = xi

    def backward(t, _):
        s = slices - 1 - t
        a_r, a_i = sandwich(
            bh[...], bl[...], waves[s + 1, 0], waves[s + 1, 1], ah[...], al[...]
        )
        w_r, w_i = waves[s, 0], waves[s, 1]
        o_r, o_i = patch[s, 0], patch[s, 1]
        patch[s, 0] = a_r * w_r + a_i * w_i
        patch[s, 1] = a_i * w_r - a_r * w_i
        waves[s, 0] = a_r * o_r + a_i * o_i
        waves[s, 1] = a_i * o_r - a_r * o_i
        return 0

    lax.fori_loop(0, slices, backward, 0)
    for out, where in ((term_s, section), (term_o, 1 - section)):
        for d in range(depth):
            for ri in range(2):
                out[ri, d] = pltpu.roll(patch[where * depth + d, ri], row, 0)


def deposit_kernel(section, rows, cols, *refs):
    pieces, (out_r, out_i) = refs[:8], refs[8:]
    n = pieces[0].shape[-1]
    span = n + 128
    row_index = lax.broadcasted_iota(jnp.int32, (n, n), 0)
    first = section[0] == 0
    for ri, out in enumerate((out_r, out_i)):
        out[...] = jnp.zeros_like(out)
        for k in range(4):
            keep = row_index >= rows[k] if k < 2 else row_index < rows[k]
            term = jnp.where(first, pieces[2 * k][ri, 0], pieces[2 * k + 1][ri, 0])
            term = jnp.where(keep, term, 0.0)
            base, shift = column_place(cols[k], out.shape[-1], span)
            wide = jnp.concatenate([term, jnp.zeros((n, 128), F32)], 1)
            out[0, :, pl.ds(base, span)] += pltpu.roll(wide, shift, 1)


def local(obj_real, obj_imag, probe, taps, intensity, row_off, col_off):
    n = probe.shape[-1]
    depth, tile, cols_all = obj_real.shape
    npos, nslab = lax.axis_size("pos"), lax.axis_size("slab")
    section = lax.axis_index("slab")

    def send(x, step, routes):
        pairs = [
            (p * nslab + src, ((p + step) % npos) * nslab + dst)
            for p in range(npos)
            for src, dst in routes
        ]
        return lax.ppermute(x, ("pos", "slab"), pairs)

    given = jnp.stack([row_off, col_off])
    tile_before = send(given, 1, ((0, 0), (1, 1)))
    order = jnp.stack([section, 1 - section])
    mine, before = given[:, order], tile_before[:, order]
    rows = jnp.concatenate([mine[0], before[0]])
    cols = jnp.concatenate([mine[1], before[1]])

    window = jax.ShapeDtypeStruct((2, depth, n, n), F32)
    window_spec = pl.BlockSpec((2, 1, n, n), lambda d: (0, d, 0, 0))
    plane_spec = pl.BlockSpec((1, tile, cols_all), lambda d: (d, 0, 0))
    anywhere = pl.BlockSpec(memory_space=pl.ANY)

    def cut(places, *after):
        count = places.shape[0]
        return pl.pallas_call(
            cut_kernel,
            grid=(depth,),
            out_shape=[window] * count,
            in_specs=[SMEM, plane_spec, plane_spec] + [anywhere] * len(after),
            out_specs=[window_spec] * count,
            compiler_params=pltpu.CompilerParams(vmem_limit_bytes=40 * 2**20),
            cost_estimate=pl.CostEstimate(flops=0, bytes_accessed=8 * 2**20, transcendentals=0),
            name="cut",
        )(places, obj_real, obj_imag, *after)

    half = (taps.shape[1] - 1) // 2
    gap = jnp.zeros((2, 2 * n - taps.shape[1]), F32)
    back = taps[:, ::-1]
    ring = jnp.concatenate(
        [
            jnp.concatenate([t[:, half:], gap, t[:, :half]], 1)
            for t in (taps, back)
        ],
        0,
    )
    bands = pl.pallas_call(
        band_kernel,
        out_shape=jax.ShapeDtypeStruct((4, 2 * n, 2 * n), BF16),
        in_specs=[VMEM],
        out_specs=VMEM,
        compiler_params=pltpu.CompilerParams(vmem_limit_bytes=40 * 2**20),
        name="band",
    )(ring)
    (first_halo,) = cut(tile_before[1, :1], bands)
    halos = [[send(first_halo, -1, ((0, 0),)), send(first_halo, -1, ((1, 0),))]]
    second_halo, own_s, own_o = cut(
        jnp.concatenate([tile_before[1, 1:], mine[1]]), first_halo
    )
    halos.append([send(second_halo, -1, ((1, 1),)), send(second_halo, -1, ((0, 1),))])
    own_o = send(own_o, 0, ((0, 1), (1, 0)))

    info = jnp.stack([section, rows[0]]).astype(jnp.int32)
    constants = fourier_blocks(n)

    def waves(phase, *after):
        return pl.pallas_call(
            functools.partial(wave_kernel, phase),
            out_shape=[window] * 2,
            in_specs=[SMEM] + [VMEM] * 11 + [anywhere] * len(after),
            out_specs=[VMEM] * 2,
            scratch_shapes=[
                pltpu.VMEM((2 * depth, 2, n, n), F32),
                pltpu.VMEM((2 * depth + 1, 2, n, n), F32),
            ],
            compiler_params=pltpu.CompilerParams(vmem_limit_bytes=48 * 2**20),
            cost_estimate=pl.CostEstimate(
                flops=(8 * depth + 4) * 24 * n**3, bytes_accessed=2**23, transcendentals=0
            ),
            name="waves",
        )(info, own_s, own_o, *halos[phase], probe, bands, intensity, *constants, *after)

    terms = [waves(0)]
    early = send(terms[0][0], 1, ((0, 0),))
    terms.append(waves(1, early))
    pieces = [[], [], [], []]
    for k, (same, other) in enumerate(terms):
        pieces[0].append(same)
        pieces[1].append(send(other, 0, ((k, 1 - k),)))
        pieces[2].append(early if k == 0 else send(same, 1, ((k, k),)))
        pieces[3].append(send(other, 1, ((k, 1 - k),)))
    for k in (1, 3):
        pieces[k].reverse()
    return pl.pallas_call(
        deposit_kernel,
        grid=(depth,),
        out_shape=[jax.ShapeDtypeStruct(obj_real.shape, F32)] * 2,
        in_specs=[SMEM] * 3 + [window_spec] * 8,
        out_specs=[plane_spec] * 2,
        compiler_params=pltpu.CompilerParams(vmem_limit_bytes=40 * 2**20),
        name="deposit",
    )(info[:1], rows, cols, *pieces[0], *pieces[1], *pieces[2], *pieces[3])


def solution(mesh):
    in_specs = (
        P(("parts", "slab"), "pos", None),
        P(("parts", "slab"), "pos", None),
        P(),
        P(),
        P(("parts", "pos"), None, None),
        P(("parts", "pos")),
        P(("parts", "pos")),
    )
    out_specs = (P(("parts", "slab"), "pos", None), P(("parts", "slab"), "pos", None))
    return jax.shard_map(local, mesh=mesh, in_specs=in_specs, out_specs=out_specs, check_vma=False)
```
